32 devices in a mesh: blk: 8 (over z, y), rep: 4 (over x, core).
Axes of the slice: x: 2, y: 2, z: 4, core: 2. Of those that a mesh axis runs over, the one named last changes fastest.
Arguments:
- image_feats: bfloat16 [16384, 1152], P(('blk', 'rep')), may hold values from -16 to 16, as said below
- text_feats: bfloat16 [16384, 1152], P(('blk', 'rep')), may hold values from -16 to 16, as said below
- head: bfloat16 [1152, 1152], replicated, may hold values from -0.1875 to 0.1875
- image_ids: int32 [16384], P(('blk', 'rep')), may hold values from 0 to 2047
- text_ids: int32 [16384], P(('blk', 'rep')), may hold values from 0 to 2047
- log_scale: float32 [1], replicated, may hold values from 3 to 3.7
- bias: float32 [1], replicated, may hold values from -3 to -1
Outputs:
- grad_image_feats: bfloat16 [16384, 1152], P(('blk', 'rep'))
- grad_text_feats: bfloat16 [16384, 1152], P(('blk', 'rep'))
- grad_head: float32 [1152, 1152], P('blk')
The draws below stay inside these ranges and needn't reach their ends.
Inputs may be any that keep to these rules, and one draw needn't show every extreme that they name: `image_feats`: row magnitudes differ from row to row. `text_feats`: row magnitudes differ from row to row.
All inputs are finite; a program needn't handle non-finite values.
Results may differ from the reference program's by a relative error of at most 0.0072.
Values may be sent and summed in bfloat16 or wider, within the bound.
A program may use at most 128 MiB of HBM per device.

```python
import jax
import jax.numpy as jnp
from jax import lax

D = 1152
TOK_DEV = 512
HOPS = 4
NIMG = 16384
ID_RANGE = 2048
N_BLK = 8
N_REP = 4


def rough_rows(key):
    noise_key, scale_key = jax.random.split(key, 2)
    row_scale = jnp.exp(jax.random.uniform(scale_key, (NIMG, 1), jnp.float32, jnp.log(0.3), jnp.log(3.0)))
    values = jnp.clip(jax.random.normal(noise_key, (NIMG, D), jnp.float32), -4.0, 4.0)
    return (values * row_scale).astype(jnp.bfloat16)


def draw_image_feats(key, part):
    key = jax.random.fold_in(key, 11)
    return rough_rows(key)


def draw_text_feats(key, part):
    key = jax.random.fold_in(key, 23)
    return rough_rows(key)


def touch_ends(entries, rng, least, largest):
    extent = entries.shape
    index_at = [jax.random.randint(jax.random.fold_in(rng, axis), (), 0, extent[axis]) for axis in range(len(extent))]
    entries = entries.at[tuple(index_at)].set(least)
    longest = extent.index(max(extent))
    index_at[longest] = (index_at[longest] + 1) % extent[longest]
    return entries.at[tuple(index_at)].set(largest)


def noise(rng, dims, scale, reach, held_as=jnp.bfloat16):
    values = scale * jax.random.normal(rng, dims, jnp.float32)
    return jnp.clip(values, min=-reach, max=reach).astype(held_as)


def setup_inputs(seed: int = 0) -> dict:
    splits = jax.random.split(jax.random.key(seed), 8)
    return {
        "image_feats": draw_image_feats(jax.random.fold_in(splits[7], 71), 0),
        "text_feats": draw_text_feats(jax.random.fold_in(splits[7], 71), 0),
        "head": noise(splits[2], (D, D), D ** -0.5, 0.1875),
        "image_ids": touch_ends(jax.random.randint(splits[3], (NIMG,), 0, ID_RANGE), jax.random.fold_in(splits[3], 1), 0, ID_RANGE - 1).astype(jnp.int32),
        "text_ids": touch_ends(jax.random.randint(splits[4], (NIMG,), 0, ID_RANGE), jax.random.fold_in(splits[4], 1), 0, ID_RANGE - 1).astype(jnp.int32),
        "log_scale": jnp.clip(jax.random.uniform(splits[5], (1,), jnp.float32, 3.0, 3.7), 3.0, 3.7),
        "bias": jnp.clip(jax.random.uniform(splits[6], (1,), jnp.float32, -3.0, -1.0), -3.0, -1.0),
    }


def unit_rows(values):
    inverse = lax.rsqrt(lax.optimization_barrier(jnp.sum(values * values, axis=-1, keepdims=True)) + 1e-06)
    return (values * inverse, inverse)

def reference(image_feats, text_feats, head, image_ids, text_ids, log_scale, bias):
    u_full = jnp.dot(image_feats, head, preferred_element_type=jnp.float32)
    x_full, inv_u = unit_rows(u_full)
    x_half = x_full.astype(jnp.bfloat16)
    y_full, inv_t = unit_rows(text_feats.astype(jnp.float32))
    y_half = y_full.astype(jnp.bfloat16)
    scale = jnp.exp(log_scale[0])
    shape4 = (N_BLK, N_REP, TOK_DEV, D)
    xb = x_half.reshape(shape4).astype(jnp.float32)
    yb = y_half.reshape(shape4)
    img_ids = image_ids.reshape(N_BLK, N_REP, TOK_DEV)
    txt_ids = text_ids.reshape(N_BLK, N_REP, TOK_DEV)
    grad_x = jnp.zeros(shape4, jnp.float32)
    grad_y = jnp.zeros(shape4, jnp.float32)
    for step in range(HOPS + 1):
        cycle_text = jnp.roll(yb, step, axis=0).astype(jnp.float32)
        cycle_ids = jnp.roll(txt_ids, step, axis=0)
        logits = scale * jnp.einsum('brid,brjd->brij', xb, cycle_text) + bias[0]
        positive = (img_ids[:, :, :, None] == cycle_ids[:, :, None, :]).astype(jnp.float32)
        coef = (scale * (jax.nn.sigmoid(logits) - positive)).astype(jnp.bfloat16).astype(jnp.float32)
        grad_x = grad_x + jnp.einsum('brij,brjd->brid', coef, cycle_text)
        part_y = jnp.einsum('brij,brid->brjd', coef, xb)
        grad_y = grad_y + jnp.roll(part_y, -step, axis=0)
    grad_x = grad_x.reshape(NIMG, D)
    grad_y = grad_y.reshape(NIMG, D)
    grad_u = (inv_u * (grad_x - x_full * lax.optimization_barrier(jnp.sum(x_full * grad_x, axis=1, keepdims=True)))).astype(jnp.bfloat16)
    grad_image = jnp.dot(grad_u, head.T, preferred_element_type=jnp.float32).astype(jnp.bfloat16)
    grad_head = jnp.dot(image_feats.T, grad_u, preferred_element_type=jnp.float32) / (N_BLK * N_REP)
    grad_text = (inv_t * (grad_y - y_full * lax.optimization_barrier(jnp.sum(y_full * grad_y, axis=1, keepdims=True)))).astype(jnp.bfloat16)
    return (grad_image, grad_text, grad_head)
```

```python
import jax
import jax.numpy as jnp
from jax import lax
from jax.sharding import PartitionSpec as P

HOPS = 4


def shifted(value, axis, steps):
    count = lax.axis_size(axis)
    pairs = [(source, (source + steps) % count) for source in range(count)]
    return lax.ppermute(value, axis, pairs)


def swapped(value, axis, bit, senders=(0, 1)):
    count = lax.axis_size(axis)
    pairs = [(k, k ^ bit) for k in range(count) if (k // bit) % 2 in senders]
    return lax.ppermute(value, axis, pairs)


def after(value, *others):
    return lax.optimization_barrier((value, *others))[0]


def unit_rows(values):
    inverse = lax.rsqrt(jnp.sum(values * values, axis=-1, keepdims=True) + 1e-06)
    return (values * inverse, inverse)


def halved(value, axis, bit, dim):
    half = value.shape[dim] // 2
    mine = (lax.axis_index(axis) // bit) % 2
    send = lax.dynamic_slice_in_dim(value, (1 - mine) * half, half, dim).astype(jnp.bfloat16)
    keep = lax.dynamic_slice_in_dim(value, mine * half, half, dim)
    return keep + swapped(send, axis, bit).astype(jnp.float32)


def head_rows(partial):
    n_blk, n_rep = lax.axis_size("blk"), lax.axis_size("rep")
    rows, columns = partial.shape
    value = partial.reshape(n_blk, rows // n_blk, columns)
    split = []
    bit = 1
    while bit < n_rep:
        if value.shape[1] % 2 == 0:
            value = halved(value, "rep", bit, 1)
            split.append(bit)
        else:
            value = value + swapped(value, "rep", bit)
        bit *= 2
    bit = n_blk // 2
    while bit >= 1:
        value = halved(value, "blk", bit, 0)
        bit //= 2
    value = value[0] / (n_blk * n_rep)
    for bit in reversed(split):
        mine = (lax.axis_index("rep") // bit) % 2
        other = swapped(value, "rep", bit)
        first = jnp.where(mine == 0, value, other)
        second = jnp.where(mine == 0, other, value)
        value = jnp.concatenate([first, second], axis=0)
    return value


def per_device(image_feats, text_feats, head, image_ids, text_ids, log_scale, bias):
    n_blk = lax.axis_size("blk")
    me = lax.axis_index("blk")
    odd = me % 2 == 1
    scale = jnp.exp(log_scale[0])
    offset = bias[0]

    y_full, inv_t = unit_rows(text_feats.astype(jnp.float32))
    y_half = y_full.astype(jnp.bfloat16)
    ids = lax.all_gather(jnp.stack([image_ids, text_ids]), "blk")

    y_back2 = shifted(y_half, "blk", 2)
    u_local = jnp.dot(image_feats, head, preferred_element_type=jnp.float32)
    x_full, inv_u = unit_rows(u_local)
    x_half = x_full.astype(jnp.bfloat16)
    own_pair = swapped(jnp.where(odd, x_half, y_half), "blk", 1)
    y_back4 = shifted(y_back2, "blk", 2)
    y_cross2 = swapped(y_back2, "blk", 1)
    y_cross4 = swapped(y_back4, "blk", 1, (1,))

    x_fore2 = shifted(after(x_half, y_back4), "blk", -2)
    x_fore4 = shifted(x_fore2, "blk", -2)
    x_cross2 = swapped(x_fore2, "blk", 1)
    x_cross4 = swapped(x_fore4, "blk", 1, (0,))

    def labels(kind, step):
        return lax.dynamic_index_in_dim(ids, (me + step + n_blk) % n_blk, 0, False)[kind]

    def coefficients(images, image_labels, texts, text_labels):
        logits = (
            scale * jnp.einsum("id,jd->ij", images, texts, preferred_element_type=jnp.float32)
            + offset
        )
        positive = (image_labels[:, None] == text_labels[None, :]).astype(jnp.float32)
        return (scale * (jax.nn.sigmoid(logits) - positive)).astype(jnp.bfloat16)

    def image_part(texts, step):
        coef = coefficients(x_half, image_ids, texts, labels(1, step))
        return jnp.dot(coef, texts, preferred_element_type=jnp.float32)

    def text_part(images, step):
        coef = coefficients(images, labels(0, step), y_half, text_ids)
        return jnp.einsum("ij,id->jd", coef, images, preferred_element_type=jnp.float32)

    own = coefficients(x_half, image_ids, y_half, text_ids)
    grad_x = jnp.dot(own, y_half, preferred_element_type=jnp.float32)
    grad_y = jnp.einsum("ij,id->jd", own, x_half, preferred_element_type=jnp.float32)

    grad_x = grad_x + image_part(y_back2, -2)
    grad_x = grad_x + image_part(y_cross2, jnp.where(odd, -3, -1))
    grad_x = grad_x + image_part(y_back4, -4)
    grad_x = grad_x + image_part(jnp.where(odd, own_pair, y_cross4), jnp.where(odd, -1, -3))

    grad_u = (inv_u * (grad_x - x_full * jnp.sum(x_full * grad_x, axis=1, keepdims=True))).astype(
        jnp.bfloat16
    )
    grad_head = head_rows(
        jnp.einsum("ie,id->ed", image_feats, grad_u, preferred_element_type=jnp.float32)
    )
    grad_image = jnp.einsum("id,ed->ie", grad_u, head, preferred_element_type=jnp.float32).astype(
        jnp.bfloat16
    )

    grad_y = grad_y + text_part(x_fore2, 2)
    grad_y = grad_y + text_part(x_cross2, jnp.where(odd, 1, 3))
    grad_y = grad_y + text_part(x_fore4, 4)
    grad_y = grad_y + text_part(jnp.where(odd, x_cross4, own_pair), jnp.where(odd, 3, 1))
    grad_text = (
        inv_t * (grad_y - y_full * jnp.sum(y_full * grad_y, axis=1, keepdims=True))
    ).astype(jnp.bfloat16)
    return (grad_image, grad_text, grad_head)


def solution(mesh):
    placed = (
        P(("blk", "rep"), None),
        P(("blk", "rep"), None),
        P(),
        P(("blk", "rep")),
        P(("blk", "rep")),
        P(),
        P(),
    )
    return jax.shard_map(
        per_device,
        mesh=mesh,
        in_specs=placed,
        out_specs=(P(("blk", "rep"), None), P(("blk", "rep"), None), P("blk", None)),
        check_vma=False,
    )
```

```python
import jax
import jax.numpy as jnp
from jax import lax
from jax.sharding import PartitionSpec as P

HOPS = 4


def shifted(value, axis, steps):
    count = lax.axis_size(axis)
    pairs = [(source, (source + steps) % count) for source in range(count)]
    return lax.ppermute(value, axis, pairs)


def swapped(value, axis, bit, senders=(0, 1)):
    count = lax.axis_size(axis)
    pairs = [(k, k ^ bit) for k in range(count) if (k // bit) % 2 in senders]
    return lax.ppermute(value, axis, pairs)


def after(value, *others):
    return lax.optimization_barrier((value, *others))[0]


def unit_rows(values):
    inverse = lax.rsqrt(jnp.sum(values * values, axis=-1, keepdims=True) + 1e-06)
    return (values * inverse, inverse)


def halved(value, axis, bit, dim):
    half = value.shape[dim] // 2
    mine = (lax.axis_index(axis) // bit) % 2
    send = lax.dynamic_slice_in_dim(value, (1 - mine) * half, half, dim).astype(jnp.bfloat16)
    keep = lax.dynamic_slice_in_dim(value, mine * half, half, dim)
    return keep + swapped(send, axis, bit).astype(jnp.float32)


def head_rows(partial, arrived):
    n_blk, n_rep = lax.axis_size("blk"), lax.axis_size("rep")
    rows, columns = partial.shape
    value = partial.reshape(n_blk, rows // n_blk, columns)
    split = []
    bit = 1
    while bit < n_rep:
        if value.shape[1] % 2 == 0:
            value = halved(value, "rep", bit, 1)
            split.append(bit)
        else:
            value = value + swapped(value, "rep", bit)
        bit *= 2
    value = after(value, arrived)
    bit = n_blk // 2
    while bit >= 1:
        value = halved(value, "blk", bit, 0)
        bit //= 2
    value = value[0] / (n_blk * n_rep)
    for bit in reversed(split):
        mine = (lax.axis_index("rep") // bit) % 2
        other = swapped(value, "rep", bit)
        first = jnp.where(mine == 0, value, other)
        second = jnp.where(mine == 0, other, value)
        value = jnp.concatenate([first, second], axis=0)
    return value


def with_ids(half, ids):
    digits = jnp.stack([ids // 256, ids % 256]).astype(half.dtype)
    digits = jnp.pad(digits, ((0, 6), (0, half.shape[1] - ids.shape[0])))
    return jnp.concatenate([half, digits], axis=0)


def split_ids(packed):
    rows = packed.shape[0] - 8
    digits = packed[rows : rows + 2, :rows].astype(jnp.float32)
    return (packed[:rows], digits[0] * 256.0 + digits[1])


def per_device(image_feats, text_feats, head, image_ids, text_ids, log_scale, bias):
    odd = lax.axis_index("blk") % 2 == 1
    scale = jnp.exp(log_scale[0])
    offset = bias[0]
    image_labels = image_ids.astype(jnp.float32)
    text_labels = text_ids.astype(jnp.float32)

    def coefficients(rows, row_labels, columns, column_labels):
        logits = (
            scale * jnp.einsum("id,jd->ij", rows, columns, preferred_element_type=jnp.float32)
            + offset
        )
        positive = (row_labels[:, None] == column_labels[None, :]).astype(jnp.float32)
        coef = (scale * (jax.nn.sigmoid(logits) - positive)).astype(jnp.bfloat16)
        return lax.optimization_barrier(coef)

    def image_part(packed):
        texts, labels = split_ids(packed)
        coef = coefficients(x_half, image_labels, texts, labels)
        return jnp.dot(coef, texts, preferred_element_type=jnp.float32)

    def text_part(packed):
        images, labels = split_ids(packed)
        coef = coefficients(y_half, text_labels, images, labels)
        return jnp.dot(coef, images, preferred_element_type=jnp.float32)

    y_full, inv_t = unit_rows(text_feats.astype(jnp.float32))
    y_half = y_full.astype(jnp.bfloat16)
    y_own = lax.optimization_barrier(with_ids(y_half, text_ids))
    y_back2 = shifted(y_own, "blk", 2)
    u_local = jnp.dot(after(image_feats, y_own), head, preferred_element_type=jnp.float32)
    x_full, inv_u = unit_rows(u_local)
    x_half = x_full.astype(jnp.bfloat16)
    x_own = with_ids(x_half, image_ids)
    own = coefficients(x_half, image_labels, y_half, text_labels)
    grad_x = jnp.dot(own, y_half, preferred_element_type=jnp.float32)
    grad_y = jnp.einsum("ij,id->jd", own, x_half, preferred_element_type=jnp.float32)
    y_back2, x_own, grad_x, grad_y = lax.optimization_barrier((y_back2, x_own, grad_x, grad_y))

    y_back4 = shifted(y_back2, "blk", 2)
    y_cross2 = swapped(y_back2, "blk", 1)
    grad_x = grad_x + image_part(y_back2)
    y_back4, y_cross2, grad_x = lax.optimization_barrier((y_back4, y_cross2, grad_x))

    x_fore2 = shifted(after(x_own, y_back4), "blk", -2)
    y_cross4 = swapped(jnp.where(odd, y_back4, y_own), "blk", 1)
    grad_x = grad_x + image_part(y_cross2)
    grad_x = grad_x + image_part(y_back4)
    x_fore2, y_cross4, grad_x = lax.optimization_barrier((x_fore2, y_cross4, grad_x))

    x_fore4 = shifted(x_fore2, "blk", -2)
    x_cross2 = swapped(x_fore2, "blk", 1)
    grad_x = lax.optimization_barrier(grad_x + image_part(y_cross4))
    grad_u = (inv_u * (grad_x - x_full * jnp.sum(x_full * grad_x, axis=1, keepdims=True))).astype(
        jnp.bfloat16
    )
    partial = jnp.einsum("ie,id->ed", image_feats, grad_u, preferred_element_type=jnp.float32)
    grad_image = jnp.einsum("id,ed->ie", grad_u, head, preferred_element_type=jnp.float32).astype(
        jnp.bfloat16
    )
    grad_y = grad_y + text_part(x_fore2)

    x_cross4 = swapped(jnp.where(odd, x_own, x_fore4), "blk", 1)
    grad_head = head_rows(partial, x_fore4)
    grad_y = grad_y + text_part(x_cross2)
    grad_y = grad_y + text_part(x_fore4)
    grad_y = lax.optimization_barrier(grad_y + text_part(x_cross4))
    grad_text = (
        inv_t * (grad_y - y_full * jnp.sum(y_full * grad_y, axis=1, keepdims=True))
    ).astype(jnp.bfloat16)
    return (grad_image, grad_text, grad_head)


def solution(mesh):
    placed = (
        P(("blk", "rep"), None),
        P(("blk", "rep"), None),
        P(),
        P(("blk", "rep")),
        P(("blk", "rep")),
        P(),
        P(),
    )
    return jax.shard_map(
        per_device,
        mesh=mesh,
        in_specs=placed,
        out_specs=(P(("blk", "rep"), None), P(("blk", "rep"), None), P("blk", None)),
        check_vma=False,
    )
```

```python
import jax
import jax.numpy as jnp
from jax import lax
from jax.sharding import PartitionSpec as P

HOPS = 4


def shifted(value, axis, steps):
    count = lax.axis_size(axis)
    pairs = [(source, (source + steps) % count) for source in range(count)]
    return lax.ppermute(value, axis, pairs)


def swapped(value, axis, bit, senders=(0, 1)):
    count = lax.axis_size(axis)
    pairs = [(k, k ^ bit) for k in range(count) if (k // bit) % 2 in senders]
    return lax.ppermute(value, axis, pairs)


def after(value, *others):
    return lax.optimization_barrier((value, *others))[0]


def unit_rows(values):
    inverse = lax.rsqrt(jnp.sum(values * values, axis=-1, keepdims=True) + 1e-06)
    return (values * inverse, inverse)


def halved(value, axis, bit, dim):
    half = value.shape[dim] // 2
    mine = (lax.axis_index(axis) // bit) % 2
    send = lax.dynamic_slice_in_dim(value, (1 - mine) * half, half, dim).astype(jnp.bfloat16)
    keep = lax.dynamic_slice_in_dim(value, mine * half, half, dim)
    return keep + swapped(send, axis, bit).astype(jnp.float32)


def head_over_rep(partial):
    n_blk, n_rep = lax.axis_size("blk"), lax.axis_size("rep")
    rows, columns = partial.shape
    value = partial.reshape(n_blk, rows // n_blk, columns)
    bits = [1 << place for place in range(n_rep.bit_length() - 1)]
    if value.shape[1] % n_rep:
        split = []
        for bit in bits:
            if value.shape[1] % 2 == 0:
                value = halved(value, "rep", bit, 1)
                split.append(bit)
            else:
                value = value + swapped(value, "rep", bit)
        return (value, split)
    share = value.shape[1] // n_rep
    me = lax.axis_index("rep")
    mine = sum(((me // bit) % 2) * (n_rep // 2 // bit) for bit in bits)
    total = lax.dynamic_slice_in_dim(value, mine * share, share, 1)
    for other in range(n_rep - 1, 0, -1):
        flips = sum(((other // bit) % 2) * (n_rep // 2 // bit) for bit in bits)
        send = lax.dynamic_slice_in_dim(value, (mine ^ flips) * share, share, 1)
        pairs = [(k, k ^ other) for k in range(n_rep)]
        total = total + lax.ppermute(send.astype(jnp.bfloat16), "rep", pairs).astype(jnp.float32)
    return (total, bits)


def head_over_blk(value, split, arrived):
    n_blk, n_rep = lax.axis_size("blk"), lax.axis_size("rep")
    share = value.shape[1:]
    n_bits = n_blk.bit_length() - 1
    value = value.reshape((2,) * n_bits + share)
    for place in list(range(1, n_bits)) + [0]:
        value = halved(value, "blk", 1 << place, n_bits - 1 - place)
    value = after(value.reshape(share) / (n_blk * n_rep), arrived)
    for bit in reversed(split):
        mine = (lax.axis_index("rep") // bit) % 2
        other = swapped(value, "rep", bit)
        first = jnp.where(mine == 0, value, other)
        second = jnp.where(mine == 0, other, value)
        value = jnp.concatenate([first, second], axis=0)
    return value


def with_ids(half, ids):
    digits = jnp.stack([ids // 256, ids % 256]).astype(half.dtype)
    digits = jnp.pad(digits, ((0, 6), (0, half.shape[1] - ids.shape[0])))
    return jnp.concatenate([half, digits], axis=0)


def split_ids(packed):
    rows = packed.shape[0] - 8
    digits = packed[rows : rows + 2, :rows].astype(jnp.float32)
    return (packed[:rows], digits[0] * 256.0 + digits[1])


def per_device(image_feats, text_feats, head, image_ids, text_ids, log_scale, bias):
    odd = lax.axis_index("blk") % 2 == 1
    scale = jnp.exp(log_scale[0])
    offset = bias[0]
    image_labels = image_ids.astype(jnp.float32)
    text_labels = text_ids.astype(jnp.float32)

    def coefficients(rows, row_labels, columns, column_labels):
        logits = (
            scale * jnp.einsum("id,jd->ij", rows, columns, preferred_element_type=jnp.float32)
            + offset
        )
        positive = (row_labels[:, None] == column_labels[None, :]).astype(jnp.float32)
        coef = (scale * (jax.nn.sigmoid(logits) - positive)).astype(jnp.bfloat16)
        return lax.optimization_barrier(coef)

    def image_part(packed):
        texts, labels = split_ids(packed)
        coef = coefficients(x_half, image_labels, texts, labels)
        return jnp.dot(coef, texts, preferred_element_type=jnp.float32)

    def text_part(packed):
        images, labels = split_ids(packed)
        coef = coefficients(y_half, text_labels, images, labels)
        return jnp.dot(coef, images, preferred_element_type=jnp.float32)

    y_full, inv_t = unit_rows(text_feats.astype(jnp.float32))
    y_half = y_full.astype(jnp.bfloat16)
    y_own = lax.optimization_barrier(with_ids(y_half, text_ids))
    y_back2 = shifted(y_own, "blk", 2)
    u_local = jnp.dot(after(image_feats, y_own), head, preferred_element_type=jnp.float32)
    x_full, inv_u = unit_rows(u_local)
    x_half = x_full.astype(jnp.bfloat16)
    x_own = with_ids(x_half, image_ids)
    own = coefficients(x_half, image_labels, y_half, text_labels)
    grad_x = jnp.dot(own, y_half, preferred_element_type=jnp.float32)
    grad_y = jnp.einsum("ij,id->jd", own, x_half, preferred_element_type=jnp.float32)
    y_back2, x_own, grad_x, grad_y = lax.optimization_barrier((y_back2, x_own, grad_x, grad_y))

    y_back4 = shifted(y_back2, "blk", 2)
    y_cross2 = swapped(y_back2, "blk", 1)
    grad_x = grad_x + image_part(y_back2)
    y_back4, y_cross2, grad_x = lax.optimization_barrier((y_back4, y_cross2, grad_x))

    x_fore2 = shifted(after(x_own, y_back4), "blk", -2)
    y_cross4 = swapped(jnp.where(odd, y_back4, y_own), "blk", 1)
    grad_x = grad_x + image_part(y_cross2)
    grad_x = grad_x + image_part(y_back4)
    x_fore2, y_cross4, grad_x = lax.optimization_barrier((x_fore2, y_cross4, grad_x))

    x_fore4 = shifted(x_fore2, "blk", -2)
    x_cross2 = swapped(x_fore2, "blk", 1)
    grad_x = lax.optimization_barrier(grad_x + image_part(y_cross4))
    grad_u = (inv_u * (grad_x - x_full * jnp.sum(x_full * grad_x, axis=1, keepdims=True))).astype(
        jnp.bfloat16
    )
    partial = jnp.einsum("ie,id->ed", image_feats, grad_u, preferred_element_type=jnp.float32)
    over_rep, split = head_over_rep(partial)
    grad_image = jnp.einsum("id,ed->ie", grad_u, head, preferred_element_type=jnp.float32).astype(
        jnp.bfloat16
    )
    grad_y = grad_y + text_part(x_fore2)

    x_fore4, x_cross2, over_rep = lax.optimization_barrier((x_fore4, x_cross2, over_rep))

    x_cross4 = swapped(jnp.where(odd, x_own, x_fore4), "blk", 1)
    grad_head = head_over_blk(over_rep, split, x_cross4)
    grad_y = grad_y + text_part(x_cross2)
    grad_y = grad_y + text_part(x_fore4)
    grad_y = lax.optimization_barrier(grad_y + text_part(x_cross4))
    grad_text = (
        inv_t * (grad_y - y_full * jnp.sum(y_full * grad_y, axis=1, keepdims=True))
    ).astype(jnp.bfloat16)
    return (grad_image, grad_text, grad_head)


def solution(mesh):
    placed = (
        P(("blk", "rep"), None),
        P(("blk", "rep"), None),
        P(),
        P(("blk", "rep")),
        P(("blk", "rep")),
        P(),
        P(),
    )
    return jax.shard_map(
        per_device,
        mesh=mesh,
        in_specs=placed,
        out_specs=(P(("blk", "rep"), None), P(("blk", "rep"), None), P("blk", None)),
        check_vma=False,
    )
```
